256 devices in a mesh: section: 32 (over z, y), dp: 8 (over x, core).
Axes of the slice: x: 4, y: 4, z: 8, core: 2. Of those that a mesh axis runs over, the one named last changes fastest.
Arguments:
- loaded: bfloat16 [1024, 2560], P(('section', 'dp')), may hold values from -6 to 6
- positions: int32 [1024], P(('section', 'dp')), may hold values from 0 to 127, as said below
- span_lengths: int32 [8, 6], P('dp'), may hold values from 1 to 32, 128 in all within a row
- visit_embed: bfloat16 [6, 2560], replicated, may hold values from -6 to 6
- w_query: bfloat16 [81920, 1280], P(('section', 'dp')), may hold values from -0.125 to 0.125
- w_key: bfloat16 [81920, 1280], P(('section', 'dp')), may hold values from -0.125 to 0.125
- w_value: bfloat16 [81920, 1280], P(('section', 'dp')), may hold values from -0.125 to 0.125
- w_out: bfloat16 [40960, 2560], P(('section', 'dp')), may hold values from -0.5 to 0.5
- norm_gain: float32 [81920], P('section'), may hold values from 0.25 to 1.75
Outputs:
- section_out: bfloat16 [32, 1024, 2560], P('section', 'dp')
The draws below stay inside these ranges and needn't reach their ends.
Inputs may be any that keep to these rules, and one draw needn't show every extreme that they name: For each history, its 128 positions appear once each among the loaded rows of its devices.
All inputs are finite; a program needn't handle non-finite values.
Results may differ from the reference program's by a relative error of at most 0.03.
Values may be sent and summed in bfloat16 or wider, within the bound.
No kernel may reach another device: no remote copies, remote signals or barrier semaphores. Data moves between devices by JAX's collectives and lax.ppermute only.
A program may use at most 128 MiB of HBM per device.

```python
import math
import jax
import jax.numpy as jnp
import numpy as np
from jax import lax

D = 2560
HEAD_DIM = 80
AHEADS = 16
ATT = 1280
LMAX = 32
NCHUNK = 6
SEQ = 128
ROWS_LOAD = 4
N_SECTION = 32
N_DP = 8


def draw_positions(key, part):
    key = jax.random.fold_in(key, 7)
    keys = jax.random.split(key, N_DP)
    perms = jax.vmap(lambda k: jax.random.permutation(k, SEQ))(keys).astype(jnp.int32)
    perms = perms.reshape(N_DP, N_SECTION, ROWS_LOAD).transpose(1, 0, 2)
    return perms.reshape(N_SECTION * N_DP * ROWS_LOAD)


def block_scale(rng, extent, shards, least, largest):
    def one(axis_at, parts):
        steps = jax.random.uniform(jax.random.fold_in(jax.random.fold_in(rng, 6), axis_at), (parts,), jnp.float32, least / len(shards), largest / len(shards))
        return jnp.repeat(jnp.exp(steps), extent[axis_at] // parts).reshape((-1,) + (1,) * (len(extent) - axis_at - 1))

    level = one(*shards[0])
    for cut in shards[1:]:
        level = level * one(*cut)
    return level


def profile(amount, total, limit, lean):
    portions = [(1 << 20) // math.isqrt(standing ** lean) + 1 for standing in range(2, amount + 1)]
    surplus, counts = total - limit - (amount - 1), [1] * (amount - 1)
    while surplus > 0:
        movable = [i for i in range(amount - 1) if counts[i] < limit]
        pool, remaining = sum([portions[i] for i in movable]), surplus
        for i in movable:
            addition = min(limit - counts[i], max(1, remaining * portions[i] // pool), surplus)
            counts[i] = counts[i] + addition
            surplus = surplus - addition
    return np.array([limit] + counts)


def uneven_parts(rng, count, total, limit, lean):
    if count == 2:
        one = jax.random.randint(rng, (), max(1, total - limit), min(limit, total - 1) + 1)
        return jnp.stack([one, total - one])
    tallies = jnp.asarray(profile(count, total, limit, lean), jnp.int32)
    pairs = (count - 1) // 2
    giver, sink = tallies[1:1 + 2 * pairs:2], tallies[2:2 + 2 * pairs:2]
    margin = jnp.minimum(giver - 1, limit - sink)
    passed = jax.random.randint(jax.random.fold_in(rng, 1), (pairs,), 0, 1 << 20) % (margin + 1)
    tallies = tallies.at[1:1 + 2 * pairs:2].set(giver - passed).at[2:2 + 2 * pairs:2].set(sink + passed)
    return tallies[jax.random.permutation(jax.random.fold_in(rng, 2), count)]


def centred(key, dims, scale, bound, pieces=(), held_as=jnp.bfloat16):
    loudness = block_scale(key, dims, pieces, -0.22, 0.18) if pieces else 1.0
    array = jax.random.normal(key, dims, jnp.float32) * scale * loudness
    return jnp.minimum(jnp.maximum(array, -bound), bound).astype(held_as)


def setup_inputs(seed: int = 0) -> dict:
    splits = jax.random.split(jax.random.key(seed), 10)
    loaded = centred(splits[0], (N_SECTION * N_DP * ROWS_LOAD, D), 1.0, 6.0, ((0, 256),))
    positions = draw_positions(jax.random.fold_in(splits[9], 71), 0)
    span_lengths = jax.vmap(lambda own: uneven_parts(own, NCHUNK, SEQ, LMAX, 2))(jax.random.split(splits[2], N_DP)).reshape((N_DP, NCHUNK)).astype(jnp.int32)
    visit_embed = centred(splits[3], (NCHUNK, D), 1.0, 6.0)
    w_query = centred(splits[4], (N_SECTION * D, ATT), D ** -0.5, 0.125, ((0, 256),))
    w_key = centred(splits[5], (N_SECTION * D, ATT), D ** -0.5, 0.125, ((0, 256),))
    w_value = centred(splits[6], (N_SECTION * D, ATT), D ** -0.5, 0.125, ((0, 256),))
    w_out = centred(splits[7], (N_SECTION * ATT, D), (ATT // 8) ** -0.5, 0.5, ((0, 256),))
    norm_gain = jnp.clip(1.0 + 0.15 * jax.random.normal(splits[8], (N_SECTION * D,), jnp.float32), 0.25, 1.75)
    return dict(loaded=loaded, positions=positions, span_lengths=span_lengths, visit_embed=visit_embed, w_query=w_query, w_key=w_key, w_value=w_value, w_out=w_out, norm_gain=norm_gain)


def layer(stream, w_query_s, w_key_s, w_value_s, w_out_s, gain, allowed):
    floats = stream.astype(jnp.float32)
    normed = (floats / jnp.sqrt(lax.optimization_barrier(jnp.mean(floats * floats, axis=1, keepdims=True)) + 1e-05) * gain).astype(jnp.bfloat16)
    query = jnp.dot(normed, w_query_s, preferred_element_type=jnp.float32).astype(jnp.bfloat16)
    keys_all = jnp.dot(normed, w_key_s, preferred_element_type=jnp.float32).astype(jnp.bfloat16)
    values_all = jnp.dot(normed, w_value_s, preferred_element_type=jnp.float32).astype(jnp.bfloat16)
    rows = stream.shape[0]
    query_heads = query.reshape(rows, AHEADS, HEAD_DIM).astype(jnp.float32)
    key_heads = keys_all.reshape(rows, AHEADS, HEAD_DIM).astype(jnp.float32)
    value_heads = values_all.reshape(rows, AHEADS, HEAD_DIM).astype(jnp.float32)
    scores = jnp.einsum('ihd,jhd->hij', query_heads, key_heads) / jnp.sqrt(jnp.float32(HEAD_DIM))
    scores = jnp.where(allowed[None], scores, -1e+30)
    probs = jax.nn.softmax(scores, axis=-1).astype(jnp.bfloat16).astype(jnp.float32)
    attended = jnp.einsum('hij,jhd->ihd', probs, value_heads).reshape(rows, ATT).astype(jnp.bfloat16)
    mixed = jnp.dot(attended, w_out_s, preferred_element_type=jnp.float32)
    return (floats + mixed).astype(jnp.bfloat16)

def reference(loaded, positions, span_lengths, visit_embed, w_query, w_key, w_value, w_out, norm_gain):
    blocks = loaded.reshape(N_SECTION, N_DP, ROWS_LOAD, D)
    where_at = positions.reshape(N_SECTION, N_DP, ROWS_LOAD)
    query_all = w_query.reshape(N_SECTION, D, ATT)
    key_all = w_key.reshape(N_SECTION, D, ATT)
    value_all = w_value.reshape(N_SECTION, D, ATT)
    out_all = w_out.reshape(N_SECTION, ATT, D)
    gains = norm_gain.reshape(N_SECTION, D)
    index_col = jnp.arange(SEQ, dtype=jnp.int32)
    allowed = index_col[None, :] <= index_col[:, None]
    outputs = []
    for group in range(N_DP):
        rows_g = blocks[:, group].reshape(SEQ, D)
        where_g = where_at[:, group].reshape(SEQ).astype(jnp.int32)
        placed = jnp.zeros((SEQ, D), jnp.bfloat16).at[where_g].set(rows_g)
        ends = jnp.cumsum(span_lengths[group]).astype(jnp.int32)
        visit_id = lax.optimization_barrier(jnp.sum((index_col[:, None] >= ends[None, :]).astype(jnp.int32), axis=1))
        start_x = (placed.astype(jnp.float32) + visit_embed[visit_id].astype(jnp.float32)).astype(jnp.bfloat16)

        def step(carry, weights):
            result = layer(carry, weights[0], weights[1], weights[2], weights[3], weights[4], allowed)
            return (result, result)
        final, per_section = lax.scan(step, start_x, (query_all, key_all, value_all, out_all, gains))
        outputs.append(per_section)
    return jnp.concatenate(outputs, axis=1)
```

```python
import jax
import jax.numpy as jnp
from jax import lax
from jax.experimental import pallas as pl
from jax.experimental.pallas import tpu as pltpu
from jax.sharding import PartitionSpec as P

HEADS = 16
GROUP = 8
ROWS = 16
SKEW = 2
BF16 = jnp.bfloat16
F32 = jnp.float32


def in_vmem(value):
    return pltpu.with_memory_space_constraint(value, pltpu.VMEM)


def in_hbm(value):
    return pltpu.with_memory_space_constraint(value, pltpu.HBM)


VMEM_SPEC = pl.BlockSpec(memory_space=pltpu.VMEM)
SMEM_SPEC = pl.BlockSpec(memory_space=pltpu.SMEM)
HBM_SPEC = pl.BlockSpec(memory_space=pltpu.HBM)


def lane_shift(chips, steps):
    return [
        (x * 2 + c, ((x + steps) % chips) * 2 + c) for x in range(chips) for c in range(2)
    ]


def load_weights(chip, core, pieces):
    offsets = [(0, 0), (0, 1), (-1, 0), (-1, 1), (1, 0), (1, 1), (2, 0), (2, 1)]
    count = len(offsets)
    part = pieces[0][0].shape[0]
    att = pieces[0][0].shape[1]
    out_part, width = pieces[3][0].shape

    def body(where, *refs):
        sources = refs[: 4 * count]
        qkv, out, sems = refs[4 * count :]
        copies = []
        for k in range(4):
            for j, (away, other) in enumerate(offsets):
                x = lax.rem(where[0] + away + 4, 4)
                c = where[1] if other == 0 else 1 - where[1]
                spot = x * 2 + c
                if k < 3:
                    target = qkv.at[pl.ds(pl.multiple_of(spot * part, part), part), pl.ds(k * att, att)]
                else:
                    target = out.at[pl.ds(pl.multiple_of(spot * out_part, out_part), out_part), :]
                copies.append(pltpu.make_async_copy(sources[k * count + j], target, sems.at[k * count + j]))
        for copy in copies:
            copy.start()
        for copy in copies:
            copy.wait()

    flat = [in_hbm(piece) for group in pieces for piece in group]
    return pl.pallas_call(
        body,
        out_shape=(
            pltpu.VMEM((part * count, 3 * att), BF16),
            pltpu.VMEM((out_part * count, width), BF16),
        ),
        in_specs=[SMEM_SPEC] + [HBM_SPEC] * len(flat),
        out_specs=[VMEM_SPEC] * 2,
        scratch_shapes=[pltpu.SemaphoreType.DMA((4 * count,))],
        compiler_params=pltpu.CompilerParams(vmem_limit_bytes=2 * 2**20),
        name="load_weights",
    )(jnp.stack([chip, core]), *flat)


def step_body(step, blocks, where, x_in, start_x, gain, qkv, out, k_in, v_in, o_in, y, keys, values, outs):
    section = where[2]
    block = step - SKEW * section
    att, width = out.shape
    seq = keys.shape[0]
    size = att // HEADS
    wide = GROUP * size

    @pl.when((block >= 0) & (block < blocks))
    def _():
        row = pl.multiple_of(block * ROWS, ROWS)
        rows = pl.ds(row, ROWS)
        first = (jnp.zeros((ROWS, width), jnp.int32) + section) == 0
        x = jnp.where(first, start_x[rows, :].astype(F32), x_in[...].astype(F32))
        normed = (
            x / jnp.sqrt(jnp.mean(x * x, axis=1, keepdims=True) + 1e-05) * gain[...]
        ).astype(BF16)
        mixed = jnp.dot(normed, qkv[...], preferred_element_type=F32).astype(BF16)
        query = mixed[:, :att]
        keys[rows, :] = mixed[:, att : 2 * att]
        values[rows, :] = mixed[:, 2 * att :]
        lane = lax.broadcasted_iota(jnp.int32, (GROUP, ROWS, wide), 2)
        head = lax.broadcasted_iota(jnp.int32, (GROUP, ROWS, wide), 0)
        own = (lane >= head * size) & (lane < (head + 1) * size)
        key_at = lax.broadcasted_iota(jnp.int32, (GROUP, ROWS, seq), 2)
        query_at = lax.broadcasted_iota(jnp.int32, (GROUP, ROWS, seq), 1) + row
        allowed = (key_at <= query_at).reshape(GROUP * ROWS, seq)
        joined = []
        for g in range(HEADS // GROUP):
            cols = slice(g * wide, (g + 1) * wide)
            spread = jnp.where(
                own, jnp.broadcast_to(query[:, cols][None], (GROUP, ROWS, wide)), jnp.zeros((), BF16)
            ).reshape(GROUP * ROWS, wide)
            scores = lax.dot_general(
                spread, keys[:, cols], (((1,), (1,)), ((), ())), preferred_element_type=F32
            )
            scores = jnp.where(allowed, scores / jnp.sqrt(F32(size)), -1e30)
            powers = jnp.exp(scores - jnp.max(scores, axis=1, keepdims=True))
            probs = (powers / jnp.sum(powers, axis=1, keepdims=True)).astype(BF16)
            mixed_v = jnp.dot(probs, values[:, cols], preferred_element_type=F32)
            mixed_v = jnp.where(own, mixed_v.reshape(GROUP, ROWS, wide), 0.0)
            joined.append(jnp.sum(mixed_v, axis=0).astype(BF16))
        attended = jnp.concatenate(joined, axis=1)
        result = (x + jnp.dot(attended, out[...], preferred_element_type=F32)).astype(BF16)
        y[...] = result
        outs[rows, :] = result


def run_step(step, blocks, where, x_in, start_x, gain, qkv, out, keys, values, outs):
    width = out.shape[1]

    def body(*refs):
        step_body(step, blocks, *refs)

    return pl.pallas_call(
        body,
        out_shape=(
            pltpu.VMEM((ROWS, width), BF16),
            pltpu.VMEM(keys.shape, BF16),
            pltpu.VMEM(values.shape, BF16),
            pltpu.VMEM(outs.shape, BF16),
        ),
        in_specs=[SMEM_SPEC] + [VMEM_SPEC] * 8,
        out_specs=[VMEM_SPEC] * 4,
        input_output_aliases={6: 1, 7: 2, 8: 3},
        compiler_params=pltpu.CompilerParams(vmem_limit_bytes=12 * 2**20),
        cost_estimate=pl.CostEstimate(flops=2**20, bytes_accessed=2**20, transcendentals=0),
        name="layer",
    )(
        where,
        in_vmem(x_in),
        in_vmem(start_x),
        in_vmem(gain),
        in_vmem(qkv),
        in_vmem(out),
        in_vmem(keys),
        in_vmem(values),
        in_vmem(outs),
    )


def shards(loaded, positions, span_lengths, visit_embed, w_query, w_key, w_value, w_out, norm_gain):
    width = loaded.shape[1]
    sections = lax.axis_size("section")
    chips = lax.axis_size("dp") // 2
    section = lax.axis_index("section")
    spot = lax.axis_index("dp")
    seq = loaded.shape[0] * sections
    att = w_query.shape[1]
    blocks = seq // ROWS

    right, left = lane_shift(chips, 1), lane_shift(chips, -1)
    sibling = [(i, i ^ 1) for i in range(2 * chips)]
    weights = [w_query, w_key, w_value, w_out]
    from_left = [lax.ppermute(w, "dp", right) for w in weights]
    from_right = [lax.ppermute(w, "dp", left) for w in weights]
    from_far = [
        lax.ppermute(from_left[k], "dp", right) if k % 2 == 0 else lax.ppermute(from_right[k], "dp", left)
        for k in range(4)
    ]
    pieces = []
    for k in range(4):
        group = []
        for piece in (weights[k], from_left[k], from_right[k], from_far[k]):
            group += [piece, lax.ppermute(piece, "dp", sibling)]
        pieces.append(group)

    tagged = jnp.concatenate(
        [loaded, jnp.broadcast_to(positions[:, None], (positions.shape[0], 128)).astype(BF16)], axis=1
    )
    gathered = lax.all_gather(tagged, "section", axis=0, tiled=True)
    owners = gathered[:, width].astype(jnp.int32)
    index = jnp.arange(seq, dtype=jnp.int32)
    placing = (index[:, None] == owners[None, :]).astype(BF16)
    ordered = jnp.dot(placing, gathered[:, :width], preferred_element_type=F32)
    lengths = span_lengths[0]
    ends = jnp.cumsum(lengths)
    visit = jnp.sum((index[:, None] >= ends[None, :]).astype(jnp.int32), axis=1)
    visit_hot = (visit[:, None] == jnp.arange(lengths.shape[0], dtype=jnp.int32)[None, :]).astype(BF16)
    start_x = (ordered + jnp.dot(visit_hot, visit_embed, preferred_element_type=F32)).astype(BF16)

    where = jnp.stack([spot // 2, spot % 2, section]).astype(jnp.int32)
    qkv, out = load_weights(spot // 2, spot % 2, pieces)
    keys = jnp.zeros((seq, att), BF16)
    values = jnp.zeros((seq, att), BF16)
    outs = jnp.zeros((seq, width), BF16)
    gain = norm_gain[None, :]
    arriving = {}
    zero = jnp.zeros((ROWS, width), BF16)
    for step in range(SKEW * (sections - 1) + blocks):
        x_in = arriving.pop(step, zero)
        y, keys, values, outs = run_step(
            step, blocks, where, x_in, start_x, gain, qkv, out, keys, values, outs
        )
        pairs = [
            (s, s + 1) for s in range(sections - 1) if 0 <= step - SKEW * s < blocks
        ]
        if pairs:
            arriving[step + SKEW] = lax.ppermute(y, "section", pairs)
    return outs[None]


def solution(mesh):
    placed = (
        P(("section", "dp"), None),
        P(("section", "dp")),
        P("dp", None),
        P(),
        P(("section", "dp"), None),
        P(("section", "dp"), None),
        P(("section", "dp"), None),
        P(("section", "dp"), None),
        P("section"),
    )
    return jax.shard_map(
        shards, mesh=mesh, in_specs=placed, out_specs=P("section", "dp", None), check_vma=False
    )
```

```python
import jax
import jax.numpy as jnp
from jax import lax
from jax.experimental import pallas as pl
from jax.experimental.pallas import tpu as pltpu
from jax.sharding import PartitionSpec as P

HEADS = 16
GROUP = 8
ROWS = 16
SKEW = 2
WINDOW = 6
BF16 = jnp.bfloat16
F32 = jnp.float32


def in_vmem(value):
    return pltpu.with_memory_space_constraint(value, pltpu.VMEM)


def in_hbm(value):
    return pltpu.with_memory_space_constraint(value, pltpu.HBM)


VMEM_SPEC = pl.BlockSpec(memory_space=pltpu.VMEM)
HBM_SPEC = pl.BlockSpec(memory_space=pltpu.HBM)


def lane_shift(chips, steps):
    return [
        (x * 2 + c, ((x + steps) % chips) * 2 + c) for x in range(chips) for c in range(2)
    ]


def load_weights(pieces, shards_in_all):
    share = sum(p.shape[0] for _, away, other, p in pieces if away == 0 and other == 0)
    width = pieces[0][3].shape[1]

    def body(*refs):
        sources = refs[: len(pieces)]
        target, sems = refs[len(pieces) :]
        spot = lax.axis_index("dp")
        chip, core = spot // 2, lax.rem(spot, 2)
        copies = []
        for i, (first, away, other, piece) in enumerate(pieces):
            x = lax.rem(chip + away + 4, 4)
            c = core if other == 0 else 1 - core
            row = pl.multiple_of((x * 2 + c) * share + first, 16)
            copies.append(
                pltpu.make_async_copy(
                    sources[i], target.at[pl.ds(row, piece.shape[0]), :], sems.at[i]
                )
            )
        for copy in copies:
            copy.start()
        for copy in copies:
            copy.wait()

    flat = [in_hbm(piece[3]) for piece in pieces]
    return pl.pallas_call(
        body,
        out_shape=pltpu.VMEM((share * shards_in_all, width), BF16),
        in_specs=[HBM_SPEC] * len(flat),
        out_specs=VMEM_SPEC,
        scratch_shapes=[pltpu.SemaphoreType.DMA((len(flat),))],
        compiler_params=pltpu.CompilerParams(vmem_limit_bytes=2 * 2**20),
        name="load_weights",
    )(*flat)


def step_body(step, blocks, x_in, start_x, gain, masks, qkv, out, k_in, v_in, o_in, y, keys, values, outs):
    section = lax.axis_index("section")
    block = step - SKEW * section
    att, width = out.shape
    seq = keys.shape[0]
    size = att // HEADS
    wide = GROUP * size

    @pl.when((block >= 0) & (block < blocks))
    def _():
        row = pl.multiple_of(block * ROWS, ROWS)
        rows = pl.ds(row, ROWS)
        first = (jnp.zeros((ROWS, width), jnp.int32) + section) == 0
        x = jnp.where(first, start_x[rows, :].astype(F32), x_in[...].astype(F32))
        normed = (
            x * lax.rsqrt(jnp.mean(x * x, axis=1, keepdims=True) + 1e-05) * gain[...]
        ).astype(BF16)
        mixed = jnp.dot(normed, qkv[...], preferred_element_type=F32).astype(BF16)
        query = mixed[:, :att]
        keys[rows, :] = mixed[:, att : 2 * att]
        values[rows, :] = mixed[:, 2 * att :]
        mask = masks[...]
        key_at = lax.broadcasted_iota(jnp.int32, (GROUP, ROWS, seq), 2)
        query_at = lax.broadcasted_iota(jnp.int32, (GROUP, ROWS, seq), 1) + row
        allowed = (key_at <= query_at).reshape(GROUP * ROWS, seq)
        joined = []
        for g in range(HEADS // GROUP):
            cols = slice(g * wide, (g + 1) * wide)
            spread = (query[:, cols][None] * mask.astype(BF16)[:, None, :]).reshape(GROUP * ROWS, wide)
            scores = lax.dot_general(
                spread, keys[:, cols], (((1,), (1,)), ((), ())), preferred_element_type=F32
            )
            scores = jnp.where(allowed, scores * (size**-0.5), -1e30)
            powers = jnp.exp(scores - jnp.max(scores, axis=1, keepdims=True))
            probs = (powers * (1.0 / jnp.sum(powers, axis=1, keepdims=True))).astype(BF16)
            mixed_v = jnp.dot(probs, values[:, cols], preferred_element_type=F32)
            mixed_v = mixed_v.reshape(GROUP, ROWS, wide) * mask[:, None, :]
            joined.append(jnp.sum(mixed_v, axis=0).astype(BF16))
        attended = jnp.concatenate(joined, axis=1)
        result = (x + jnp.dot(attended, out[...], preferred_element_type=F32)).astype(BF16)
        y[...] = result
        outs[rows, :] = result


def run_step(step, blocks, x_in, start_x, gain, masks, qkv, out, keys, values, outs):
    width = out.shape[1]

    def body(*refs):
        step_body(step, blocks, *refs)

    operands = (x_in, start_x, gain, masks, qkv, out, keys, values, outs)
    return pl.pallas_call(
        body,
        out_shape=(
            pltpu.VMEM((ROWS, width), BF16),
            pltpu.VMEM(keys.shape, BF16),
            pltpu.VMEM(values.shape, BF16),
            pltpu.VMEM(outs.shape, BF16),
        ),
        in_specs=[VMEM_SPEC] * len(operands),
        out_specs=[VMEM_SPEC] * 4,
        input_output_aliases={6: 1, 7: 2, 8: 3},
        compiler_params=pltpu.CompilerParams(vmem_limit_bytes=12 * 2**20),
        cost_estimate=pl.CostEstimate(flops=2**20, bytes_accessed=2**20, transcendentals=0),
        name="layer",
    )(*[in_vmem(operand) for operand in operands])


def after(value, *events):
    return lax.optimization_barrier((value, *events))[0]


def shards(loaded, positions, span_lengths, visit_embed, w_query, w_key, w_value, w_out, norm_gain):
    width = loaded.shape[1]
    sections = lax.axis_size("section")
    chips = lax.axis_size("dp") // 2
    seq = loaded.shape[0] * sections
    att = w_query.shape[1]
    blocks = seq // ROWS

    right, left = lane_shift(chips, 1), lane_shift(chips, -1)
    sibling = [(i, i ^ 1) for i in range(2 * chips)]
    shares = (jnp.concatenate([w_query, w_key, w_value], axis=1), w_out)
    from_left = [lax.ppermute(share, "dp", right) for share in shares]
    from_right = [lax.ppermute(share, "dp", left) for share in shares]
    others = [None, lax.ppermute(w_out, "dp", sibling)]

    tagged = jnp.concatenate(
        [loaded, jnp.broadcast_to(positions[:, None], (positions.shape[0], 128)).astype(BF16)], axis=1
    )
    gathered = lax.all_gather(after(tagged, others[1]), "section", axis=0, tiled=True)
    owners = gathered[:, width].astype(jnp.int32)
    index = jnp.arange(seq, dtype=jnp.int32)
    placing = (index[:, None] == owners[None, :]).astype(BF16)
    ordered = jnp.dot(placing, gathered[:, :width], preferred_element_type=F32)
    lengths = span_lengths[0]
    ends = jnp.cumsum(lengths)
    visit = jnp.sum((index[:, None] >= ends[None, :]).astype(jnp.int32), axis=1)
    visit_hot = (visit[:, None] == jnp.arange(lengths.shape[0], dtype=jnp.int32)[None, :]).astype(BF16)
    start_x = (ordered + jnp.dot(visit_hot, visit_embed, preferred_element_type=F32)).astype(BF16)

    loaded_weights = []
    for k, share in enumerate(shares):
        half = share.shape[0] // 2
        far = [
            (0, 2, lax.ppermute(after(from_left[k][:half], start_x), "dp", right)),
            (half, 2, lax.ppermute(after(from_right[k][half:], start_x), "dp", left)),
        ]
        pieces = []
        for first, away, got in ((0, 0, share), (0, -1, from_left[k]), (0, 1, from_right[k]), *far):
            other = others[k] if away == 0 else None
            if other is None:
                other = lax.ppermute(after(got, start_x), "dp", sibling)
            pieces.append((first, away, 0, got))
            pieces.append((first, away, 1, other))
        loaded_weights.append(load_weights(pieces, 2 * chips))

    wide = GROUP * (att // HEADS)
    masks = (
        jnp.arange(wide, dtype=jnp.int32)[None, :] // (att // HEADS)
        == jnp.arange(GROUP, dtype=jnp.int32)[:, None]
    ).astype(F32)
    qkv, out = loaded_weights
    keys = jnp.zeros((seq, att), BF16)
    values = jnp.zeros((seq, att), BF16)
    outs = jnp.zeros((seq, width), BF16)
    gain = norm_gain[None, :]
    arriving = {}
    nothing = jnp.zeros((ROWS, width), BF16)
    last = SKEW * (sections - 1) + blocks
    for step in range(last):
        x_in = arriving.pop(step, nothing)
        y, keys, values, outs = run_step(
            step, blocks, x_in, start_x, gain, masks, qkv, out, keys, values, outs
        )
        if step + SKEW < last:
            base = step // WINDOW * WINDOW
            pairs = [
                (s, s + 1)
                for s in range(sections - 1)
                if any(0 <= t - SKEW * s < blocks for t in range(base, base + WINDOW))
            ]
            arriving[step + SKEW] = lax.ppermute(y, "section", pairs)
    return outs[None]


def solution(mesh):
    placed = (
        P(("section", "dp"), None),
        P(("section", "dp")),
        P("dp", None),
        P(),
        P(("section", "dp"), None),
        P(("section", "dp"), None),
        P(("section", "dp"), None),
        P(("section", "dp"), None),
        P("section"),
    )
    return jax.shard_map(
        shards, mesh=mesh, in_specs=placed, out_specs=P("section", "dp", None), check_vma=False
    )
```

```python
import jax
import jax.numpy as jnp
from jax import lax
from jax.experimental import pallas as pl
from jax.experimental.pallas import tpu as pltpu
from jax.sharding import PartitionSpec as P

HEADS = 16
GROUP = 8
LANES = 128
WINDOWS = ((0, (0, 1, 2)), (1, (3,)), (2, (4, 5)), (3, (6, 7)))
ROWS = 16
SKEW = 2
BF16 = jnp.bfloat16
F32 = jnp.float32


def in_vmem(value):
    return pltpu.with_memory_space_constraint(value, pltpu.VMEM)


def in_hbm(value):
    return pltpu.with_memory_space_constraint(value, pltpu.HBM)


VMEM_SPEC = pl.BlockSpec(memory_space=pltpu.VMEM)
HBM_SPEC = pl.BlockSpec(memory_space=pltpu.HBM)


def lane_shift(chips, steps):
    return [
        (x * 2 + c, ((x + steps) % chips) * 2 + c) for x in range(chips) for c in range(2)
    ]


def load_weights(pieces, shards_in_all):
    share = sum(p.shape[0] for _, away, other, p in pieces if away == 0 and other == 0)
    width = pieces[0][3].shape[1]

    def body(*refs):
        sources = refs[: len(pieces)]
        target, sems = refs[len(pieces) :]
        spot = lax.axis_index("dp")
        chip, core = spot // 2, lax.rem(spot, 2)
        copies = []
        for i, (first, away, other, piece) in enumerate(pieces):
            x = lax.rem(chip + away + 4, 4)
            c = core if other == 0 else 1 - core
            row = pl.multiple_of((x * 2 + c) * share + first, 16)
            copies.append(
                pltpu.make_async_copy(
                    sources[i], target.at[pl.ds(row, piece.shape[0]), :], sems.at[i]
                )
            )
        for copy in copies:
            copy.start()
        for copy in copies:
            copy.wait()

    flat = [in_hbm(piece[3]) for piece in pieces]
    return pl.pallas_call(
        body,
        out_shape=pltpu.VMEM((share * shards_in_all, width), BF16),
        in_specs=[HBM_SPEC] * len(flat),
        out_specs=VMEM_SPEC,
        scratch_shapes=[pltpu.SemaphoreType.DMA((len(flat),))],
        compiler_params=pltpu.CompilerParams(vmem_limit_bytes=2 * 2**20),
        name="load_weights",
    )(*flat)


def step_body(step, blocks, x_in, start_x, gain, masks, qkv, out, k_in, v_in, o_in, y, keys, values, outs):
    section = lax.axis_index("section")
    block = step - SKEW * section
    att, width = out.shape
    seq = keys.shape[0]
    size = att // HEADS
    wide = GROUP * size

    @pl.when((block >= 0) & (block < blocks))
    def _():
        row = pl.multiple_of(block * ROWS, ROWS)
        rows = pl.ds(row, ROWS)
        first = (jnp.zeros((ROWS, width), jnp.int32) + section) == 0
        x = jnp.where(first, start_x[rows, :].astype(F32), x_in[...].astype(F32))
        normed = (
            x * lax.rsqrt(jnp.mean(x * x, axis=1, keepdims=True) + 1e-05) * gain[...]
        ).astype(BF16)
        mixed = jnp.dot(normed, qkv[...], preferred_element_type=F32).astype(BF16)
        query = mixed[:, :att]
        keys[rows, :] = mixed[:, att : 2 * att]
        values[rows, :] = mixed[:, 2 * att :]
        mask = masks[...]
        low = mask.astype(BF16)
        scores = []
        for base in range(0, att, wide):
            for tile, heads in WINDOWS:
                cols = slice(base + tile * LANES, base + (tile + 2) * LANES)
                own = low[heads[0] : heads[-1] + 1]
                spread = (query[:, cols][None] * own[:, None, :]).reshape(-1, 2 * LANES)
                scores.append(
                    lax.dot_general(
                        spread, keys[:, cols], (((1,), (1,)), ((), ())), preferred_element_type=F32
                    )
                )
        scores = jnp.concatenate(scores, axis=0)
        key_at = lax.broadcasted_iota(jnp.int32, (HEADS, ROWS, seq), 2)
        query_at = lax.broadcasted_iota(jnp.int32, (HEADS, ROWS, seq), 1) + row
        allowed = (key_at <= query_at).reshape(HEADS * ROWS, seq)
        scores = jnp.where(allowed, scores * (size**-0.5), -1e30)
        powers = jnp.exp(scores - jnp.max(scores, axis=1, keepdims=True))
        probs = (powers * (1.0 / jnp.sum(powers, axis=1, keepdims=True))).astype(BF16)
        joined = []
        at = 0
        for base in range(0, att, wide):
            tiles = [None] * (wide // LANES)
            for tile, heads in WINDOWS:
                cols = slice(base + tile * LANES, base + (tile + 2) * LANES)
                own = mask[heads[0] : heads[-1] + 1]
                count = len(heads)
                part = jnp.dot(
                    probs[at : at + count * ROWS], values[:, cols], preferred_element_type=F32
                )
                at += count * ROWS
                part = jnp.sum(part.reshape(count, ROWS, 2 * LANES) * own[:, None, :], axis=0)
                for j in range(2):
                    piece = part[:, j * LANES : (j + 1) * LANES]
                    held = tiles[tile + j]
                    tiles[tile + j] = piece if held is None else held + piece
            joined += [tile.astype(BF16) for tile in tiles]
        attended = jnp.concatenate(joined, axis=1)
        result = (x + jnp.dot(attended, out[...], preferred_element_type=F32)).astype(BF16)
        y[...] = result
        outs[rows, :] = result


def run_step(step, blocks, x_in, start_x, gain, masks, qkv, out, keys, values, outs):
    width = out.shape[1]

    def body(*refs):
        step_body(step, blocks, *refs)

    operands = (x_in, start_x, gain, masks, qkv, out, keys, values, outs)
    return pl.pallas_call(
        body,
        out_shape=(
            pltpu.VMEM((ROWS, width), BF16),
            pltpu.VMEM(keys.shape, BF16),
            pltpu.VMEM(values.shape, BF16),
            pltpu.VMEM(outs.shape, BF16),
        ),
        in_specs=[VMEM_SPEC] * len(operands),
        out_specs=[VMEM_SPEC] * 4,
        input_output_aliases={6: 1, 7: 2, 8: 3},
        compiler_params=pltpu.CompilerParams(vmem_limit_bytes=12 * 2**20),
        cost_estimate=pl.CostEstimate(flops=2**20, bytes_accessed=2**20, transcendentals=0),
        name="layer",
    )(*[in_vmem(operand) for operand in operands])


def after(value, *events):
    return lax.optimization_barrier((value, *events))[0]


def shards(loaded, positions, span_lengths, visit_embed, w_query, w_key, w_value, w_out, norm_gain):
    width = loaded.shape[1]
    sections = lax.axis_size("section")
    chips = lax.axis_size("dp") // 2
    seq = loaded.shape[0] * sections
    att = w_query.shape[1]
    blocks = seq // ROWS

    right, left = lane_shift(chips, 1), lane_shift(chips, -1)
    sibling = [(i, i ^ 1) for i in range(2 * chips)]
    shares = (jnp.concatenate([w_query, w_key, w_value], axis=1), w_out)
    from_left = [lax.ppermute(share, "dp", right) for share in shares]
    from_right = [lax.ppermute(share, "dp", left) for share in shares]
    others = [None, lax.ppermute(w_out, "dp", sibling)]

    tagged = jnp.concatenate(
        [loaded, jnp.broadcast_to(positions[:, None], (positions.shape[0], 128)).astype(BF16)], axis=1
    )
    gathered = lax.all_gather(after(tagged, others[1]), "section", axis=0, tiled=True)
    owners = gathered[:, width].astype(jnp.int32)
    index = jnp.arange(seq, dtype=jnp.int32)
    placing = (index[:, None] == owners[None, :]).astype(BF16)
    ordered = jnp.dot(placing, gathered[:, :width], preferred_element_type=F32)
    lengths = span_lengths[0]
    ends = jnp.cumsum(lengths)
    visit = jnp.sum((index[:, None] >= ends[None, :]).astype(jnp.int32), axis=1)
    visit_hot = (visit[:, None] == jnp.arange(lengths.shape[0], dtype=jnp.int32)[None, :]).astype(BF16)
    start_x = (ordered + jnp.dot(visit_hot, visit_embed, preferred_element_type=F32)).astype(BF16)

    loaded_weights = []
    for k, share in enumerate(shares):
        half = share.shape[0] // 2
        far = [
            (0, 2, lax.ppermute(after(from_left[k][:half], start_x), "dp", right)),
            (half, 2, lax.ppermute(after(from_right[k][half:], start_x), "dp", left)),
        ]
        pieces = []
        for first, away, got in ((0, 0, share), (0, -1, from_left[k]), (0, 1, from_right[k]), *far):
            other = others[k] if away == 0 else None
            if other is None:
                other = lax.ppermute(after(got, start_x), "dp", sibling)
            pieces.append((first, away, 0, got))
            pieces.append((first, away, 1, other))
        loaded_weights.append(load_weights(pieces, 2 * chips))

    firsts = [0] * GROUP
    for tile, heads in WINDOWS:
        for head in heads:
            firsts[head] = tile * LANES
    lane = jnp.arange(2 * LANES, dtype=jnp.int32)[None, :] + jnp.array(firsts, jnp.int32)[:, None]
    masks = (lane // (att // HEADS) == jnp.arange(GROUP, dtype=jnp.int32)[:, None]).astype(F32)
    qkv, out = loaded_weights
    keys = jnp.zeros((seq, att), BF16)
    values = jnp.zeros((seq, att), BF16)
    outs = jnp.zeros((seq, width), BF16)
    gain = norm_gain[None, :]
    arriving = {}
    nothing = jnp.zeros((ROWS, width), BF16)
    last = SKEW * (sections - 1) + blocks
    for step in range(last):
        x_in = arriving.pop(step, nothing)
        y, keys, values, outs = run_step(
            step, blocks, x_in, start_x, gain, masks, qkv, out, keys, values, outs
        )
        if step + SKEW < last:
            pairs = [(s, (s + 1) % sections) for s in range(sections)]
            arriving[step + SKEW] = lax.ppermute(y, "section", pairs)
    return outs[None]


def solution(mesh):
    placed = (
        P(("section", "dp"), None),
        P(("section", "dp")),
        P("dp", None),
        P(),
        P(("section", "dp"), None),
        P(("section", "dp"), None),
        P(("section", "dp"), None),
        P(("section", "dp"), None),
        P("section"),
    )
    return jax.shard_map(
        shards, mesh=mesh, in_specs=placed, out_specs=P("section", "dp", None), check_vma=False
    )
```

```python
import jax
import jax.numpy as jnp
from jax import lax
from jax.experimental import pallas as pl
from jax.experimental.pallas import tpu as pltpu
from jax.sharding import PartitionSpec as P

HEADS = 16
GROUP = 8
LANES = 128
WINDOWS = ((0, (0, 1, 2)), (1, (3,)), (2, (4, 5)), (3, (6, 7)))
ROWS = 16
SKEW = 2
BF16 = jnp.bfloat16
F32 = jnp.float32


def in_vmem(value):
    return pltpu.with_memory_space_constraint(value, pltpu.VMEM)


def in_hbm(value):
    return pltpu.with_memory_space_constraint(value, pltpu.HBM)


VMEM_SPEC = pl.BlockSpec(memory_space=pltpu.VMEM)
ANY_SPEC = pl.BlockSpec(memory_space=pl.ANY)


def lane_shift(chips, steps):
    return [
        (x * 2 + c, ((x + steps) % chips) * 2 + c) for x in range(chips) for c in range(2)
    ]


def pack(w_query, w_key, w_value, w_out):
    rows, att = w_query.shape
    half = rows // 2

    def body(query, key, value, out, packed, sems):
        copies = [
            pltpu.make_async_copy(ref, packed.at[:, pl.ds(i * att, att)], sems.at[i])
            for i, ref in enumerate((query, key, value))
        ]
        copies += [
            pltpu.make_async_copy(
                out.at[:, pl.ds(i * att, att)],
                packed.at[pl.ds(i * half, half), pl.ds(3 * att, att)],
                sems.at[3 + i],
            )
            for i in range(2)
        ]
        for copy in copies:
            copy.start()
        for copy in copies:
            copy.wait()

    return pl.pallas_call(
        body,
        out_shape=jax.ShapeDtypeStruct((rows, 4 * att), BF16),
        in_specs=[ANY_SPEC] * 4,
        out_specs=ANY_SPEC,
        scratch_shapes=[pltpu.SemaphoreType.DMA((5,))],
        compiler_params=pltpu.CompilerParams(vmem_limit_bytes=2**20),
        name="pack",
    )(*[in_hbm(w) for w in (w_query, w_key, w_value, w_out)])


def load_weights(pieces, rows, shards_in_all, held=None):
    att = pieces[0][3].shape[1] // 4
    half = rows // 2
    moves = []
    for i, (first, _, _, piece) in enumerate(pieces):
        moves.append((i, 0, piece.shape[0], first, None))
        for j in range(first // half, (first + piece.shape[0]) // half):
            moves.append((i, j * half - first, half, 0, j))

    def body(*refs):
        qkv, out, sems = refs[-3:]
        spot = lax.axis_index("dp")
        chip, core = spot // 2, lax.rem(spot, 2)
        copies = []
        for m, (i, begin, count, first, side) in enumerate(moves):
            _, away, other, _ = pieces[i]
            x = lax.rem(chip + away + 4, 4)
            c = core if other == 0 else 1 - core
            owner = x * 2 + c
            if side is None:
                source = refs[i].at[:, pl.ds(0, 3 * att)]
                target = qkv.at[pl.ds(pl.multiple_of(owner * rows + first, 16), count), :]
            else:
                source = refs[i].at[pl.ds(begin, count), pl.ds(3 * att, att)]
                row = pl.multiple_of(owner * half, 16)
                target = out.at[pl.ds(row, count), pl.ds(side * att, att)]
            copies.append(pltpu.make_async_copy(source, target, sems.at[m]))
        for copy in copies:
            copy.start()
        for copy in copies:
            copy.wait()

    operands = [in_hbm(piece[3]) for piece in pieces]
    specs = [ANY_SPEC] * len(operands)
    aliases = {}
    if held is not None:
        aliases = {len(operands): 0, len(operands) + 1: 1}
        operands += [in_vmem(array) for array in held]
        specs += [VMEM_SPEC] * 2
    return pl.pallas_call(
        body,
        out_shape=(
            pltpu.VMEM((rows * shards_in_all, 3 * att), BF16),
            pltpu.VMEM((half * shards_in_all, 2 * att), BF16),
        ),
        in_specs=specs,
        out_specs=[VMEM_SPEC] * 2,
        input_output_aliases=aliases,
        scratch_shapes=[pltpu.SemaphoreType.DMA((len(moves),))],
        compiler_params=pltpu.CompilerParams(vmem_limit_bytes=2 * 2**20),
        name="load_weights",
    )(*operands)


def step_body(step, blocks, x_in, start_x, gain, masks, qkv, out, k_in, v_in, o_in, y, keys, values, outs):
    section = lax.axis_index("section")
    block = step - SKEW * section
    att, width = out.shape
    seq = keys.shape[0]
    size = att // HEADS
    wide = GROUP * size

    @pl.when((block >= 0) & (block < blocks))
    def _():
        row = pl.multiple_of(block * ROWS, ROWS)
        rows = pl.ds(row, ROWS)
        first = (jnp.zeros((ROWS, width), jnp.int32) + section) == 0
        x = jnp.where(first, start_x[rows, :].astype(F32), x_in[...].astype(F32))
        normed = (
            x * lax.rsqrt(jnp.mean(x * x, axis=1, keepdims=True) + 1e-05) * gain[...]
        ).astype(BF16)
        mixed = jnp.dot(normed, qkv[...], preferred_element_type=F32).astype(BF16)
        query = mixed[:, :att]
        keys[rows, :] = mixed[:, att : 2 * att]
        values[rows, :] = mixed[:, 2 * att :]
        mask = masks[...]
        low = mask.astype(BF16)
        scores = []
        for base in range(0, att, wide):
            for tile, heads in WINDOWS:
                cols = slice(base + tile * LANES, base + (tile + 2) * LANES)
                own = low[heads[0] : heads[-1] + 1]
                spread = (query[:, cols][None] * own[:, None, :]).reshape(-1, 2 * LANES)
                scores.append(
                    lax.dot_general(
                        spread, keys[:, cols], (((1,), (1,)), ((), ())), preferred_element_type=F32
                    )
                )
        scores = jnp.concatenate(scores, axis=0)
        key_at = lax.broadcasted_iota(jnp.int32, (HEADS, ROWS, seq), 2)
        query_at = lax.broadcasted_iota(jnp.int32, (HEADS, ROWS, seq), 1) + row
        allowed = (key_at <= query_at).reshape(HEADS * ROWS, seq)
        scores = jnp.where(allowed, scores * (size**-0.5), -1e30)
        powers = jnp.exp(scores - jnp.max(scores, axis=1, keepdims=True))
        probs = (powers * (1.0 / jnp.sum(powers, axis=1, keepdims=True))).astype(BF16)
        joined = []
        at = 0
        for base in range(0, att, wide):
            tiles = [None] * (wide // LANES)
            for tile, heads in WINDOWS:
                cols = slice(base + tile * LANES, base + (tile + 2) * LANES)
                own = mask[heads[0] : heads[-1] + 1]
                count = len(heads)
                part = jnp.dot(
                    probs[at : at + count * ROWS], values[:, cols], preferred_element_type=F32
                )
                at += count * ROWS
                part = jnp.sum(part.reshape(count, ROWS, 2 * LANES) * own[:, None, :], axis=0)
                for j in range(2):
                    piece = part[:, j * LANES : (j + 1) * LANES]
                    held = tiles[tile + j]
                    tiles[tile + j] = piece if held is None else held + piece
            joined += [tile.astype(BF16) for tile in tiles]
        attended = jnp.concatenate(joined, axis=1)
        result = (x + jnp.dot(attended, out[...], preferred_element_type=F32)).astype(BF16)
        y[...] = result
        outs[rows, :] = result


def run_step(step, blocks, x_in, start_x, gain, masks, qkv, out, keys, values, outs):
    width = out.shape[1]

    def body(*refs):
        step_body(step, blocks, *refs)

    operands = (x_in, start_x, gain, masks, qkv, out, keys, values, outs)
    return pl.pallas_call(
        body,
        out_shape=(
            pltpu.VMEM((ROWS, width), BF16),
            pltpu.VMEM(keys.shape, BF16),
            pltpu.VMEM(values.shape, BF16),
            pltpu.VMEM(outs.shape, BF16),
        ),
        in_specs=[VMEM_SPEC] * len(operands),
        out_specs=[VMEM_SPEC] * 4,
        input_output_aliases={6: 1, 7: 2, 8: 3},
        compiler_params=pltpu.CompilerParams(vmem_limit_bytes=12 * 2**20),
        cost_estimate=pl.CostEstimate(flops=2**20, bytes_accessed=2**20, transcendentals=0),
        name="layer",
    )(*[in_vmem(operand) for operand in operands])


def after(value, *events):
    return lax.optimization_barrier((value, *events))[0]


def shards(loaded, positions, span_lengths, visit_embed, w_query, w_key, w_value, w_out, norm_gain):
    width = loaded.shape[1]
    sections = lax.axis_size("section")
    chips = lax.axis_size("dp") // 2
    seq = loaded.shape[0] * sections
    att = w_query.shape[1]
    blocks = seq // ROWS

    right, left = lane_shift(chips, 1), lane_shift(chips, -1)
    sibling = [(i, i ^ 1) for i in range(2 * chips)]
    share = pack(w_query, w_key, w_value, w_out)
    from_left = lax.ppermute(share, "dp", right)
    from_right = lax.ppermute(share, "dp", left)
    under_way = lax.ppermute(share[:16, :LANES], "dp", sibling)

    tagged = jnp.concatenate(
        [loaded, jnp.broadcast_to(positions[:, None], (positions.shape[0], 128)).astype(BF16)], axis=1
    )
    gathered = lax.all_gather(after(tagged, under_way), "section", axis=0, tiled=True)
    owners = gathered[:, width].astype(jnp.int32)
    index = jnp.arange(seq, dtype=jnp.int32)
    placing = (index[:, None] == owners[None, :]).astype(BF16)
    ordered = jnp.dot(placing, gathered[:, :width], preferred_element_type=F32)
    lengths = span_lengths[0]
    ends = jnp.cumsum(lengths)
    visit = jnp.sum((index[:, None] >= ends[None, :]).astype(jnp.int32), axis=1)
    visit_hot = (visit[:, None] == jnp.arange(lengths.shape[0], dtype=jnp.int32)[None, :]).astype(BF16)
    start_x = (ordered + jnp.dot(visit_hot, visit_embed, preferred_element_type=F32)).astype(BF16)

    half = share.shape[0] // 2
    far = (
        (0, lax.ppermute(after(from_left[:half], start_x), "dp", right)),
        (half, lax.ppermute(after(from_right[half:], start_x), "dp", left)),
    )
    pieces = []
    for away, got in ((0, share), (-1, from_left), (1, from_right)):
        other = lax.ppermute(after(got, start_x), "dp", sibling)
        pieces += [(0, away, 0, got), (0, away, 1, other)]
    near = load_weights(pieces, share.shape[0], 2 * chips)
    pieces = []
    for first, got in far:
        other = lax.ppermute(after(got, near[0]), "dp", sibling)
        pieces += [(first, 2, 0, got), (first, 2, 1, other)]
    qkv, out = load_weights(pieces, share.shape[0], 2 * chips, near)

    firsts = [0] * GROUP
    for tile, heads in WINDOWS:
        for head in heads:
            firsts[head] = tile * LANES
    lane = jnp.arange(2 * LANES, dtype=jnp.int32)[None, :] + jnp.array(firsts, jnp.int32)[:, None]
    masks = (lane // (att // HEADS) == jnp.arange(GROUP, dtype=jnp.int32)[:, None]).astype(F32)
    keys = jnp.zeros((seq, att), BF16)
    values = jnp.zeros((seq, att), BF16)
    outs = jnp.zeros((seq, width), BF16)
    gain = norm_gain[None, :]
    arriving = {}
    nothing = jnp.zeros((ROWS, width), BF16)
    last = SKEW * (sections - 1) + blocks
    for step in range(last):
        x_in = arriving.pop(step, nothing)
        y, keys, values, outs = run_step(
            step, blocks, x_in, start_x, gain, masks, qkv, out, keys, values, outs
        )
        if step + SKEW < last:
            pairs = [(s, (s + 1) % sections) for s in range(sections)]
            arriving[step + SKEW] = lax.ppermute(y, "section", pairs)
    return outs[None]


def solution(mesh):
    placed = (
        P(("section", "dp"), None),
        P(("section", "dp")),
        P("dp", None),
        P(),
        P(("section", "dp"), None),
        P(("section", "dp"), None),
        P(("section", "dp"), None),
        P(("section", "dp"), None),
        P("section"),
    )
    return jax.shard_map(
        shards, mesh=mesh, in_specs=placed, out_specs=P("section", "dp", None), check_vma=False
    )
```

```python
import jax
import jax.numpy as jnp
from jax import lax
from jax.experimental import pallas as pl
from jax.experimental.pallas import tpu as pltpu
from jax.sharding import PartitionSpec as P

HEADS = 16
GROUP = 8
LANES = 128
WINDOWS = ((0, (0, 1, 2)), (1, (3,)), (2, (4, 5)), (3, (6, 7)))
ROWS = 16
SKEW = 2
BF16 = jnp.bfloat16
F32 = jnp.float32


def in_vmem(value):
    return pltpu.with_memory_space_constraint(value, pltpu.VMEM)


def in_hbm(value):
    return pltpu.with_memory_space_constraint(value, pltpu.HBM)


VMEM_SPEC = pl.BlockSpec(memory_space=pltpu.VMEM)
ANY_SPEC = pl.BlockSpec(memory_space=pl.ANY)


def lane_shift(chips, steps):
    return [
        (x * 2 + c, ((x + steps) % chips) * 2 + c) for x in range(chips) for c in range(2)
    ]


def pack(w_query, w_key, w_value, w_out):
    rows, att = w_query.shape
    half = rows // 2

    def body(query, key, value, out, packed, sems):
        copies = [
            pltpu.make_async_copy(ref, packed.at[:, pl.ds(i * att, att)], sems.at[i])
            for i, ref in enumerate((query, key, value))
        ]
        copies += [
            pltpu.make_async_copy(
                out.at[:, pl.ds(i * att, att)],
                packed.at[pl.ds(i * half, half), pl.ds(3 * att, att)],
                sems.at[3 + i],
            )
            for i in range(2)
        ]
        for copy in copies:
            copy.start()
        for copy in copies:
            copy.wait()

    return pl.pallas_call(
        body,
        out_shape=jax.ShapeDtypeStruct((rows, 4 * att), BF16),
        in_specs=[ANY_SPEC] * 4,
        out_specs=ANY_SPEC,
        scratch_shapes=[pltpu.SemaphoreType.DMA((5,))],
        compiler_params=pltpu.CompilerParams(vmem_limit_bytes=2**20),
        name="pack",
    )(*[in_hbm(w) for w in (w_query, w_key, w_value, w_out)])


def load_weights(pieces, rows, shards_in_all, held=None):
    att = pieces[0][3].shape[1] // 4
    half = rows // 2
    moves = []
    for i, (first, _, _, piece) in enumerate(pieces):
        moves.append((i, 0, piece.shape[0], first, None))
        for j in range(first // half, (first + piece.shape[0]) // half):
            moves.append((i, j * half - first, half, 0, j))

    def body(*refs):
        qkv, out, sems = refs[-3:]
        spot = lax.axis_index("dp")
        chip, core = spot // 2, lax.rem(spot, 2)
        copies = []
        for m, (i, begin, count, first, side) in enumerate(moves):
            _, away, other, _ = pieces[i]
            x = lax.rem(chip + away + 4, 4)
            c = core if other == 0 else 1 - core
            owner = x * 2 + c
            if side is None:
                source = refs[i].at[:, pl.ds(0, 3 * att)]
                target = qkv.at[pl.ds(pl.multiple_of(owner * rows + first, 16), count), :]
            else:
                source = refs[i].at[pl.ds(begin, count), pl.ds(3 * att, att)]
                row = pl.multiple_of(owner * half, 16)
                target = out.at[pl.ds(row, count), pl.ds(side * att, att)]
            copies.append(pltpu.make_async_copy(source, target, sems.at[m]))
        for copy in copies:
            copy.start()
        for copy in copies:
            copy.wait()

    operands = [in_hbm(piece[3]) for piece in pieces]
    specs = [ANY_SPEC] * len(operands)
    aliases = {}
    if held is not None:
        aliases = {len(operands): 0, len(operands) + 1: 1}
        operands += [in_vmem(array) for array in held]
        specs += [VMEM_SPEC] * 2
    return pl.pallas_call(
        body,
        out_shape=(
            pltpu.VMEM((rows * shards_in_all, 3 * att), BF16),
            pltpu.VMEM((half * shards_in_all, 2 * att), BF16),
        ),
        in_specs=specs,
        out_specs=[VMEM_SPEC] * 2,
        input_output_aliases=aliases,
        scratch_shapes=[pltpu.SemaphoreType.DMA((len(moves),))],
        compiler_params=pltpu.CompilerParams(vmem_limit_bytes=2 * 2**20),
        name="load_weights",
    )(*operands)


def step_body(step, blocks, x_in, start_x, gain, masks, qkv, out, k_in, v_in, o_in, y, keys, values, outs):
    section = lax.axis_index("section")
    block = step - SKEW * section
    att, width = out.shape
    seq = keys.shape[0]
    size = att // HEADS
    wide = GROUP * size

    @pl.when((block >= 0) & (block < blocks))
    def _():
        row = pl.multiple_of(block * ROWS, ROWS)
        rows = pl.ds(row, ROWS)
        first = (jnp.zeros((ROWS, width), jnp.int32) + section) == 0
        x = jnp.where(first, start_x[rows, :].astype(F32), x_in[...].astype(F32))
        normed = (
            x * lax.rsqrt(jnp.mean(x * x, axis=1, keepdims=True) + 1e-05) * gain[...]
        ).astype(BF16)
        mixed = jnp.dot(normed, qkv[...], preferred_element_type=F32).astype(BF16)
        query = mixed[:, :att]
        keys[rows, :] = mixed[:, att : 2 * att]
        values[rows, :] = mixed[:, 2 * att :]
        mask = masks[...]
        low = mask.astype(BF16)
        scores = []
        for base in range(0, att, wide):
            for tile, heads in WINDOWS:
                cols = slice(base + tile * LANES, base + (tile + 2) * LANES)
                own = low[heads[0] : heads[-1] + 1]
                spread = (query[:, cols][None] * own[:, None, :]).reshape(-1, 2 * LANES)
                scores.append(
                    lax.dot_general(
                        spread, keys[:, cols], (((1,), (1,)), ((), ())), preferred_element_type=F32
                    )
                )
        scores = jnp.concatenate(scores, axis=0)
        key_at = lax.broadcasted_iota(jnp.int32, (HEADS, ROWS, seq), 2)
        query_at = lax.broadcasted_iota(jnp.int32, (HEADS, ROWS, seq), 1) + row
        allowed = (key_at <= query_at).reshape(HEADS * ROWS, seq)
        scores = jnp.where(allowed, scores * (size**-0.5), -1e30)
        powers = jnp.exp(scores - jnp.max(scores, axis=1, keepdims=True))
        probs = (powers * (1.0 / jnp.sum(powers, axis=1, keepdims=True))).astype(BF16)
        joined = []
        at = 0
        for base in range(0, att, wide):
            tiles = [None] * (wide // LANES)
            for tile, heads in WINDOWS:
                cols = slice(base + tile * LANES, base + (tile + 2) * LANES)
                own = mask[heads[0] : heads[-1] + 1]
                count = len(heads)
                part = jnp.dot(
                    probs[at : at + count * ROWS], values[:, cols], preferred_element_type=F32
                )
                at += count * ROWS
                part = jnp.sum(part.reshape(count, ROWS, 2 * LANES) * own[:, None, :], axis=0)
                for j in range(2):
                    piece = part[:, j * LANES : (j + 1) * LANES]
                    held = tiles[tile + j]
                    tiles[tile + j] = piece if held is None else held + piece
            joined += [tile.astype(BF16) for tile in tiles]
        attended = jnp.concatenate(joined, axis=1)
        result = (x + jnp.dot(attended, out[...], preferred_element_type=F32)).astype(BF16)
        y[...] = result
        outs[rows, :] = result


def run_step(step, blocks, x_in, start_x, gain, masks, qkv, out, keys, values, outs):
    width = out.shape[1]

    def body(*refs):
        step_body(step, blocks, *refs)

    operands = (x_in, start_x, gain, masks, qkv, out, keys, values, outs)
    return pl.pallas_call(
        body,
        out_shape=(
            pltpu.VMEM((ROWS, width), BF16),
            pltpu.VMEM(keys.shape, BF16),
            pltpu.VMEM(values.shape, BF16),
            pltpu.VMEM(outs.shape, BF16),
        ),
        in_specs=[VMEM_SPEC] * len(operands),
        out_specs=[VMEM_SPEC] * 4,
        input_output_aliases={6: 1, 7: 2, 8: 3},
        compiler_params=pltpu.CompilerParams(vmem_limit_bytes=12 * 2**20),
        cost_estimate=pl.CostEstimate(flops=2**20, bytes_accessed=2**20, transcendentals=0),
        name="layer",
    )(*[in_vmem(operand) for operand in operands])


def after(value, *events):
    return lax.optimization_barrier((value, *events))[0]


def shards(loaded, positions, span_lengths, visit_embed, w_query, w_key, w_value, w_out, norm_gain):
    width = loaded.shape[1]
    sections = lax.axis_size("section")
    chips = lax.axis_size("dp") // 2
    seq = loaded.shape[0] * sections
    att = w_query.shape[1]
    blocks = seq // ROWS

    right, left = lane_shift(chips, 1), lane_shift(chips, -1)
    sibling = [(i, i ^ 1) for i in range(2 * chips)]
    share = pack(w_query, w_key, w_value, w_out)
    from_left = lax.ppermute(share, "dp", right)
    from_right = lax.ppermute(share, "dp", left)
    under_way = lax.ppermute(share[:16, :LANES], "dp", sibling)

    tagged = jnp.concatenate(
        [loaded, jnp.broadcast_to(positions[:, None], (positions.shape[0], 128)).astype(BF16)], axis=1
    )
    gathered = lax.all_gather(after(tagged, under_way), "section", axis=0, tiled=True)
    owners = gathered[:, width].astype(jnp.int32)
    index = jnp.arange(seq, dtype=jnp.int32)
    placing = (index[:, None] == owners[None, :]).astype(BF16)
    ordered = jnp.dot(placing, gathered[:, :width], preferred_element_type=F32)
    lengths = span_lengths[0]
    ends = jnp.cumsum(lengths)
    visit = jnp.sum((index[:, None] >= ends[None, :]).astype(jnp.int32), axis=1)
    visit_hot = (visit[:, None] == jnp.arange(lengths.shape[0], dtype=jnp.int32)[None, :]).astype(BF16)
    start_x = (ordered + jnp.dot(visit_hot, visit_embed, preferred_element_type=F32)).astype(BF16)

    half = share.shape[0] // 2
    far = (
        (0, lax.ppermute(after(from_left[:half], start_x), "dp", right)),
        (half, lax.ppermute(after(from_right[half:], start_x), "dp", left)),
    )
    pieces = []
    for away, got in ((0, share), (-1, from_left), (1, from_right)):
        other = lax.ppermute(after(got, start_x), "dp", sibling)
        pieces += [(0, away, 0, got), (0, away, 1, other)]
    held = load_weights(pieces, share.shape[0], 2 * chips)
    for first, got in far:
        other = lax.ppermute(after(got, held[0]), "dp", sibling)
        pieces = [(first, 2, 0, got), (first, 2, 1, other)]
        held = load_weights(pieces, share.shape[0], 2 * chips, held)
    qkv, out = held

    firsts = [0] * GROUP
    for tile, heads in WINDOWS:
        for head in heads:
            firsts[head] = tile * LANES
    lane = jnp.arange(2 * LANES, dtype=jnp.int32)[None, :] + jnp.array(firsts, jnp.int32)[:, None]
    masks = (lane // (att // HEADS) == jnp.arange(GROUP, dtype=jnp.int32)[:, None]).astype(F32)
    keys = jnp.zeros((seq, att), BF16)
    values = jnp.zeros((seq, att), BF16)
    outs = jnp.zeros((seq, width), BF16)
    gain = norm_gain[None, :]
    arriving = {}
    nothing = jnp.zeros((ROWS, width), BF16)
    last = SKEW * (sections - 1) + blocks
    for step in range(last):
        x_in = arriving.pop(step, nothing)
        y, keys, values, outs = run_step(
            step, blocks, x_in, start_x, gain, masks, qkv, out, keys, values, outs
        )
        if step + SKEW < last:
            pairs = [(s, (s + 1) % sections) for s in range(sections)]
            arriving[step + SKEW] = lax.ppermute(y, "section", pairs)
    return outs[None]


def solution(mesh):
    placed = (
        P(("section", "dp"), None),
        P(("section", "dp")),
        P("dp", None),
        P(),
        P(("section", "dp"), None),
        P(("section", "dp"), None),
        P(("section", "dp"), None),
        P(("section", "dp"), None),
        P("section"),
    )
    return jax.shard_map(
        shards, mesh=mesh, in_specs=placed, out_specs=P("section", "dp", None), check_vma=False
    )
```
